32 devices in a mesh: groups: 2 (over y), views: 4 (over z), cols: 2 (over x), sub: 2 (over core).
Axes of the slice: x: 2, y: 2, z: 4, core: 2. Of those that a mesh axis runs over, the one named last changes fastest.
Arguments:
- images: bfloat16 [32, 8, 256], P(('groups', 'views'), None, 'cols'), parts along dimension 0, may hold values from -6 to 6
- pairs: int32 [128, 2], P('groups'), parts along dimension 0, may hold values from 0 to 15, as said below
- offsets: int32 [128], P('groups'), parts along dimension 0, may hold values from 4 to 67
Outputs:
- volume: float32 [32, 64, 8, 256], P(('groups', 'views'), 'sub', None, 'cols'), parts along dimension 0
The draws below stay inside these ranges and needn't reach their ends.
There are 2 independent parts, one for each index of `groups`. The reference program is written for one: setup_inputs(seed, part) draws one part's arguments, and reference() takes and returns one part's arrays. A program takes and returns all parts, laid end to end along the dimension named above; each array names one. Nothing has to cross between parts.
Inputs may be any that keep to these rules, and one draw needn't show every extreme that they name: `pairs`: rows b * 16 to (b + 1) * 16 - 1 name as first view one of views b * 4 to (b + 1) * 4 - 1. The two views of a pair differ. Among the rows of one such block, at most 8 name second views on one index of views (second view // 4), and some block reaches 8. Over all rows, at most 32 name second views on one index of views, and some index reaches 32.
All inputs are finite; a program needn't handle non-finite values.
Results may differ from the reference program's by a relative error of at most 0.00096.
Values may be sent and summed in bfloat16 or wider, within the bound.
A program may use at most 64 MiB of HBM per device.

```python
import jax
import jax.numpy as jnp
from jax import lax

V_DEV = 4
ROWS = 8
NDISP = 64
RAD = 4
OFFSPAN = 64
PAIRS_DEV = 16
VIEWS = 16
WIDTH = 256
PAIRS = 64


def draw_pairs(key, part):
    blocks = PAIRS // PAIRS_DEV
    slots_per = 2 * PAIRS_DEV // blocks
    subkeys = jax.random.split(jax.random.fold_in(key, 17), 7)
    hot_owner = jax.random.randint(subkeys[0], (), 0, blocks)
    rotation = jax.random.randint(subkeys[1], (), 0, blocks - 1)
    block_ids = jnp.arange(blocks)[:, None]
    groups_of = (jnp.arange(PAIRS_DEV) // slots_per)[None, :]
    group_class = jnp.broadcast_to(groups_of - 1, (blocks, PAIRS_DEV))
    spread = hot_owner + 1 + (block_ids + group_class + rotation) % (blocks - 1)
    owner_ids = jnp.where(group_class < 0, hot_owner, spread) % blocks
    scores = jax.random.randint(subkeys[3], (blocks, PAIRS_DEV), 0, 1048576) * PAIRS_DEV + jnp.arange(PAIRS_DEV)[None, :]
    shuffle = jnp.argsort(scores, axis=1)
    owner_ids = jnp.take_along_axis(owner_ids, shuffle, axis=1)
    first_local = jax.random.randint(subkeys[4], (blocks, PAIRS_DEV), 0, V_DEV)
    second_local = jax.random.randint(subkeys[5], (blocks, PAIRS_DEV), 0, V_DEV)
    other_local = (first_local + 1 + jax.random.randint(subkeys[6], (blocks, PAIRS_DEV), 0, V_DEV - 1)) % V_DEV
    second_local = jnp.where(owner_ids == block_ids, other_local, second_local)
    first_view = block_ids * V_DEV + first_local
    second_view = owner_ids * V_DEV + second_local
    return jnp.stack([first_view, second_view], axis=-1).reshape(PAIRS, 2).astype(jnp.int32)


def plant(entries, stream_key, least, top_value):
    shape = entries.shape
    index_at = [jax.random.randint(jax.random.fold_in(stream_key, axis), (), 0, shape[axis]) for axis in range(len(shape))]
    entries = entries.at[tuple(index_at)].set(least)
    longest = shape.index(max(shape))
    index_at[longest] = (index_at[longest] + 1) % shape[longest]
    return entries.at[tuple(index_at)].set(top_value)


def level_of(own_key, extent, cuts, smallest, largest):
    def one(position, parts):
        steps = jax.random.uniform(jax.random.fold_in(jax.random.fold_in(own_key, 6), position), (parts,), jnp.float32, smallest / len(cuts), largest / len(cuts))
        return jnp.repeat(jnp.exp(steps), extent[position] // parts).reshape((-1,) + (1,) * (len(extent) - position - 1))

    gain = one(*cuts[0])
    for cut in cuts[1:]:
        gain = gain * one(*cut)
    return gain


def bell_draw(stream_key, shape, deviation, most, cuts=(), held_as=jnp.bfloat16):
    level = level_of(stream_key, shape, cuts, -0.22, 0.18) if cuts else 1.0
    array = jax.random.normal(stream_key, shape, jnp.float32) * deviation * level
    return jnp.minimum(jnp.maximum(array, -most), most).astype(held_as)


def setup_inputs(seed: int = 0, part: int = 0) -> dict:
    streams_of = jax.random.split(jax.random.key(seed), 4)
    part_splits = jax.random.split(jax.random.fold_in(streams_of[3], part), 4)
    images = bell_draw(part_splits[0], (VIEWS, ROWS, WIDTH), 1.0, 6.0, ((0, 4), (2, 2)))
    pairs = draw_pairs(jax.random.fold_in(jax.random.fold_in(streams_of[3], part), 71), part)
    offsets = plant(jax.random.randint(part_splits[2], (PAIRS,), RAD, RAD + OFFSPAN), jax.random.fold_in(part_splits[2], 1), RAD, (RAD + OFFSPAN) - 1).astype(jnp.int32)
    return {"images": images, "pairs": pairs, "offsets": offsets}


SMOOTH = 0.01

def box_sum(values, radius):
    row_count = values.shape[-2]
    columns = values.shape[-1] - 2 * radius
    widths = [(0, 0)] * (values.ndim - 2) + [(radius, radius), (0, 0)]
    padded = jnp.pad(values, widths)
    row_sums = padded[..., 0:row_count, :]
    for offset_row in range(1, 2 * radius + 1):
        row_sums = row_sums + padded[..., offset_row:offset_row + row_count, :]
    column_sums = row_sums[..., 0:columns]
    for offset_col in range(1, 2 * radius + 1):
        column_sums = column_sums + row_sums[..., offset_col:offset_col + columns]
    return column_sums

def pair_costs(window, strip_cols, disp_count, radius):
    span_cols = window.shape[-1]
    shifted = jnp.stack([strip_cols[:, disp_count - 1 - shift_index:disp_count - 1 - shift_index + span_cols] for shift_index in range(disp_count)])
    inverse = 1.0 / float((2 * radius + 1) ** 2)
    mean_first = box_sum(window, radius) * inverse
    power_first = box_sum(window * window, radius) * inverse
    mean_second = box_sum(shifted, radius) * inverse
    power_second = box_sum(shifted * shifted, radius) * inverse
    cross_term = box_sum(window[None] * shifted, radius) * inverse
    spread_first = power_first - mean_first * mean_first + SMOOTH
    spread_second = power_second - mean_second * mean_second + SMOOTH
    cost_block = 1.0 - (cross_term - mean_first * mean_second) / jnp.sqrt(spread_first * spread_second)
    return cost_block.astype(jnp.bfloat16)

def reference(images, pairs, offsets):
    view_count, row_count, columns = images.shape
    lead_cols = 2 * RAD + OFFSPAN + NDISP
    padded = jnp.pad(images.astype(jnp.float32), ((0, 0), (0, 0), (lead_cols, RAD)))
    strip_len = columns + 2 * RAD + NDISP - 1

    def accumulate(volume, members):
        pair_row, shift_value = members
        first_tile = lax.dynamic_index_in_dim(padded, pair_row[0], 0, keepdims=False)
        second_tile = lax.dynamic_index_in_dim(padded, pair_row[1], 0, keepdims=False)
        window = first_tile[:, lead_cols - RAD:lead_cols + columns + RAD]
        first_col = (lead_cols - RAD - NDISP + 1 - shift_value).astype(jnp.int32)
        strip_cols = lax.dynamic_slice_in_dim(second_tile, first_col, strip_len, 1)
        cost_block = pair_costs(window, strip_cols, NDISP, RAD).astype(jnp.float32)
        volume = volume.at[pair_row[0]].add(cost_block)
        volume = volume.at[pair_row[1]].add(cost_block)
        return (volume, None)
    volume = jnp.zeros((view_count, NDISP, row_count, columns), jnp.float32)
    volume, unused = lax.scan(accumulate, volume, (pairs, offsets))
    return volume
```

```python
import functools

import jax
import jax.numpy as jnp
from jax import lax
from jax.experimental import pallas as pl
from jax.experimental.pallas import tpu as pltpu
from jax.sharding import PartitionSpec as P

NDISP = 64
RAD = 4
SMOOTH = 0.01
LANES = 128
WIN = 2 * RAD + 1
MESH = pl.DeviceIdType.MESH


def gather_kernel(blocks, cols, x_ref, out_ref, send_sem, recv_sem, own_sem):
    my_view = lax.axis_index("views")
    my_col = lax.axis_index("cols")
    me = my_view * cols + my_col
    total = blocks * cols

    def peer(step):
        other = lax.rem(me + step, total)
        return {"views": other // cols, "cols": lax.rem(other, cols)}

    own = pltpu.make_async_copy(x_ref, out_ref.at[my_col, my_view], own_sem)
    own.start()
    barrier = pltpu.get_barrier_semaphore()
    for step in range(1, total):
        pl.semaphore_signal(barrier, inc=1, device_id=peer(step), device_id_type=MESH)
    pl.semaphore_wait(barrier, total - 1)
    copies = []
    for step in range(1, total):
        copy = pltpu.make_async_remote_copy(
            src_ref=x_ref,
            dst_ref=out_ref.at[my_col, my_view],
            send_sem=send_sem.at[step],
            recv_sem=recv_sem.at[step],
            device_id=peer(step),
            device_id_type=MESH,
        )
        copy.start()
        copies.append(copy)
    own.wait()
    for copy in copies:
        copy.wait()


def gather_images(images, blocks, cols):
    rows, columns = images.shape
    total = blocks * cols
    return pl.pallas_call(
        functools.partial(gather_kernel, blocks, cols),
        out_shape=jax.ShapeDtypeStruct((cols, blocks, rows, columns), images.dtype),
        in_specs=[pl.BlockSpec(memory_space=pltpu.VMEM)],
        out_specs=pl.BlockSpec(memory_space=pltpu.VMEM),
        scratch_shapes=[
            pltpu.SemaphoreType.DMA((total,)),
            pltpu.SemaphoreType.DMA((total,)),
            pltpu.SemaphoreType.DMA,
        ],
        compiler_params=pltpu.CompilerParams(collective_id=0, has_side_effects=True),
    )(images)


def split_exact(values):
    high = values.astype(jnp.bfloat16)
    low = (values - high.astype(jnp.float32)).astype(jnp.bfloat16)
    return high, low


def cost_kernel(
    dims, gath_ref, pairs_ref, offs_ref, out_ref,
    nat, nat_f, nat_m, nat_r, st_g, st_m, st_r, st_f, st_a, st_b,
    gt, m2t, r2t, ft, m1t, r1t, sel, box, two, four, task_ref,
):
    blocks, cols, views, rows, columns, pair_count, per_sub, batches = dims
    per_batch = LANES // rows
    per_block = pair_count // blocks
    all_rows = blocks * views * rows
    wide = 4 * columns
    my_view = lax.axis_index("views")
    my_col = lax.axis_index("cols")
    sub_start = lax.axis_index("sub") * per_sub
    scale = 1.0 / float(WIN * WIN)

    def clear(slot, carry):
        task_ref[slot] = -1
        return carry

    lax.fori_loop(per_block, batches * per_batch, clear, 0)
    for slot in range(per_block):
        task_ref[slot] = my_view * per_block + slot

    def list_pair(pair, count):
        first = pairs_ref[2 * pair] // views
        second = pairs_ref[2 * pair + 1] // views
        take = (second == my_view) & (first != my_view)

        @pl.when(take)
        def _():
            task_ref[count] = pair

        return count + take.astype(jnp.int32)

    lax.fori_loop(0, pair_count, list_pair, jnp.int32(per_block))

    for place in range(4):
        index = my_col + (place - 2)
        ok = (index >= 0) & (index < cols)
        block = gath_ref[jnp.clip(index, 0, cols - 1)]
        block = block.reshape(all_rows, columns).astype(jnp.float32)
        nat[:, place * columns : (place + 1) * columns] = jnp.where(ok, block, 0.0)

    row_of = lax.broadcasted_iota(jnp.int32, (LANES, LANES), 0)
    lane_of = lax.broadcasted_iota(jnp.int32, (LANES, LANES), 1)
    band = (
        ((row_of // rows) == (lane_of // rows)) & (jnp.abs(row_of - lane_of) <= RAD)
    ).astype(jnp.bfloat16)
    band_wide = jnp.concatenate([band, band], axis=1)
    band_tall = jnp.concatenate([band, band], axis=0)

    def across(sums):
        pair_sum = sums + pltpu.roll(sums, 1, 1)
        quad = pair_sum + pltpu.roll(pair_sum, 2, 1)
        octo = quad + pltpu.roll(quad, 4, 1)
        return pltpu.roll(octo + pltpu.roll(sums, 8, 1), wide - RAD, 1)

    for chunk in range(all_rows // LANES):
        span = slice(chunk * LANES, (chunk + 1) * LANES)
        tile = nat[span, :]
        nat_f[span, :] = pltpu.roll(tile, 2 * columns + RAD, 1)[:, : 2 * columns]
        mean = across(
            jnp.dot(band, tile.astype(jnp.bfloat16), preferred_element_type=jnp.float32)
        ) * scale
        high, low = split_exact(tile * tile)
        power = across(
            jnp.dot(
                band_wide, jnp.concatenate([high, low], axis=0), preferred_element_type=jnp.float32
            )
        ) * scale
        nat_m[span, :] = mean
        nat_r[span, :] = lax.rsqrt(power - mean * mean + SMOOTH)

    slot_lane = lax.broadcasted_iota(jnp.int32, (views * rows, LANES), 1)
    view_row = lax.broadcasted_iota(jnp.int32, (views * rows, LANES), 0)

    def prepare(batch, carry):
        first_of = jnp.full((views * rows, LANES), -1, jnp.int32)
        second_of = first_of
        for slot in range(per_batch):
            pair = task_ref[batch * per_batch + slot]
            live = pair >= 0
            pair = jnp.maximum(pair, 0)
            first = pairs_ref[2 * pair]
            second = pairs_ref[2 * pair + 1]
            shift = offs_ref[pair]
            first_at = pl.ds(pl.multiple_of(first * rows, rows), rows)
            second_at = pl.ds(pl.multiple_of(second * rows, rows), rows)
            here = slice(slot * rows, (slot + 1) * rows)
            start = 2 * columns - per_sub - RAD - shift - sub_start
            turn = wide - start
            st_g[here, :] = pltpu.roll(nat[second_at, :], turn, 1)[:, : 2 * columns]
            st_m[here, :] = pltpu.roll(nat_m[second_at, :], turn, 1)[:, : 2 * columns]
            st_r[here, :] = pltpu.roll(nat_r[second_at, :], turn, 1)[:, : 2 * columns]
            st_f[here, :] = nat_f[first_at, :]
            st_a[here, :] = nat_m[first_at, 2 * columns : 3 * columns]
            st_b[here, :] = nat_r[first_at, 2 * columns : 3 * columns]
            mine = (slot_lane // rows) == slot
            base = my_view * views
            first_of = jnp.where(mine, jnp.where(live, first - base, -1), first_of)
            second_of = jnp.where(mine, jnp.where(live, second - base, -1), second_of)
        target = view_row // rows
        same_row = lax.rem(slot_lane, rows) == lax.rem(view_row, rows)
        hit = ((first_of == target) | (second_of == target)) & same_row
        sel[batch] = hit.astype(jnp.bfloat16)
        gt[batch] = st_g[...].T
        m2t[batch] = st_m[...].T
        r2t[batch] = st_r[...].T
        ft[batch] = st_f[...].T
        m1t[batch] = st_a[...].T * float(WIN * WIN)
        r1t[batch] = st_b[...].T * scale
        return carry

    lax.fori_loop(0, batches, prepare, 0)

    span = columns + 2 * RAD

    def score(disp, carry):
        summed = jnp.zeros((views * rows, columns), jnp.float32)
        for batch in range(batches):
            product = ft[batch, 0:span, :] * gt[batch, pl.ds(per_sub - disp, span), :]
            high, low = split_exact(product)
            sums = jnp.dot(
                jnp.concatenate([high, low], axis=1), band_tall, preferred_element_type=jnp.float32
            )
            box[batch, 0:span, :] = sums
            two[batch, 0:span, :] = sums + box[batch, 1 : span + 1, :]
            four[batch, 0:span, :] = two[batch, 0:span, :] + two[batch, 2 : span + 2, :]
            cross = (
                four[batch, 0:columns, :] + four[batch, 4 : columns + 4, :]
                + box[batch, 8 : columns + 8, :]
            )
            at = pl.ds(per_sub + RAD - disp, columns)
            gain = r1t[batch] * r2t[batch, at, :]
            cost = 1.0 - (cross - m1t[batch] * m2t[batch, at, :]) * gain
            summed = summed + lax.dot_general(
                sel[batch], cost.astype(jnp.bfloat16), (((1,), (1,)), ((), ())),
                preferred_element_type=jnp.float32,
            )
        out_ref[:, disp] = summed.reshape(views, rows, columns)
        return carry

    lax.fori_loop(0, per_sub, score, 0)


def per_device(images, pairs, offsets):
    views, rows, columns = images.shape
    blocks = lax.axis_size("views")
    cols = lax.axis_size("cols")
    per_sub = NDISP // lax.axis_size("sub")
    pair_count = pairs.shape[0]
    per_block = pair_count // blocks
    arriving = (2 * per_block // blocks) * (blocks - 1)
    per_batch = LANES // rows
    batches = -(-(per_block + arriving) // per_batch)
    gathered = gather_images(images.reshape(views * rows, columns), blocks, cols)
    dims = (blocks, cols, views, rows, columns, pair_count, per_sub, batches)
    all_rows = blocks * views * rows
    span = columns + 2 * RAD
    f32 = jnp.float32
    stage = pltpu.VMEM((LANES, 2 * columns), f32)
    narrow = pltpu.VMEM((LANES, columns), f32)
    turned = pltpu.VMEM((batches, 2 * columns, LANES), f32)
    turned_narrow = pltpu.VMEM((batches, columns, LANES), f32)
    work = pltpu.VMEM((batches, span + 8, LANES), f32)
    whole = pltpu.VMEM((all_rows, 4 * columns), f32)
    smem = pl.BlockSpec(memory_space=pltpu.SMEM)
    vmem = pl.BlockSpec(memory_space=pltpu.VMEM)
    return pl.pallas_call(
        functools.partial(cost_kernel, dims),
        out_shape=jax.ShapeDtypeStruct((views, per_sub, rows, columns), f32),
        in_specs=[vmem, smem, smem],
        out_specs=vmem,
        scratch_shapes=[
            whole, pltpu.VMEM((all_rows, 2 * columns), f32), whole, whole,
            stage, stage, stage, stage, narrow, narrow,
            turned, turned, turned, turned, turned_narrow, turned_narrow,
            pltpu.VMEM((batches, views * rows, LANES), jnp.bfloat16),
            work, work, work,
            pltpu.SMEM((batches * per_batch,), jnp.int32),
        ],
        compiler_params=pltpu.CompilerParams(vmem_limit_bytes=40 * 2**20),
    )(gathered, pairs.reshape(-1), offsets)


def solution(mesh):
    return jax.shard_map(
        per_device,
        mesh=mesh,
        in_specs=(P(("groups", "views"), None, "cols"), P("groups", None), P("groups")),
        out_specs=P(("groups", "views"), "sub", None, "cols"),
        check_vma=False,
    )
```

```python
import functools

import jax
import jax.numpy as jnp
from jax import lax
from jax.experimental import pallas as pl
from jax.experimental.pallas import tpu as pltpu
from jax.sharding import PartitionSpec as P

NDISP = 64
RAD = 4
SMOOTH = 0.01
LANES = 128
FOLD = 2
WIN = 2 * RAD + 1
MESH = pl.DeviceIdType.MESH


def gather_kernel(blocks, cols, x_ref, out_ref, send_sem, recv_sem, own_sem):
    my_view = lax.axis_index("views")
    my_col = lax.axis_index("cols")
    me = my_view * cols + my_col
    total = blocks * cols

    def peer(step):
        other = lax.rem(me + step, total)
        return {"views": other // cols, "cols": lax.rem(other, cols)}

    own = pltpu.make_async_copy(x_ref, out_ref.at[my_col, my_view], own_sem)
    own.start()
    barrier = pltpu.get_barrier_semaphore()
    for step in range(1, total):
        pl.semaphore_signal(barrier, inc=1, device_id=peer(step), device_id_type=MESH)
    pl.semaphore_wait(barrier, total - 1)
    copies = []
    for step in range(1, total):
        copy = pltpu.make_async_remote_copy(
            src_ref=x_ref,
            dst_ref=out_ref.at[my_col, my_view],
            send_sem=send_sem.at[step],
            recv_sem=recv_sem.at[step],
            device_id=peer(step),
            device_id_type=MESH,
        )
        copy.start()
        copies.append(copy)
    own.wait()
    for copy in copies:
        copy.wait()


def gather_images(images, blocks, cols):
    rows, columns = images.shape
    total = blocks * cols
    return pl.pallas_call(
        functools.partial(gather_kernel, blocks, cols),
        out_shape=jax.ShapeDtypeStruct((cols, blocks, rows, columns), images.dtype),
        in_specs=[pl.BlockSpec(memory_space=pltpu.VMEM)],
        out_specs=pl.BlockSpec(memory_space=pltpu.VMEM),
        scratch_shapes=[
            pltpu.SemaphoreType.DMA((total,)),
            pltpu.SemaphoreType.DMA((total,)),
            pltpu.SemaphoreType.DMA,
        ],
        compiler_params=pltpu.CompilerParams(collective_id=0, has_side_effects=True),
    )(images)


def split_exact(values):
    high = values.astype(jnp.bfloat16)
    low = (values - high.astype(jnp.float32)).astype(jnp.bfloat16)
    return high, low


def cost_kernel(
    dims, gath_ref, pairs_ref, offs_ref, out_ref,
    nat, nat_f, nat_m, nat_r, st_g, st_m, st_r, st_f, st_a, st_b,
    gt, m2t, r2t, ft, m1t, r1t, sel, box, two, four, task_ref,
):
    blocks, cols, views, rows, columns, pair_count, per_sub, batches, folded = dims
    per_batch = LANES // rows
    per_block = pair_count // blocks
    slots = batches * per_batch
    all_rows = blocks * views * rows
    wide = 4 * columns
    my_view = lax.axis_index("views")
    my_col = lax.axis_index("cols")
    sub_start = lax.axis_index("sub") * per_sub
    scale = 1.0 / float(WIN * WIN)

    base = my_view * views
    for slot in range(per_block):
        task_ref[slot] = my_view * per_block + slot

    def is_mine(view):
        return (view >= base) & (view < base + views)

    def list_pair(pair, count):
        take = is_mine(pairs_ref[1, pair]) & jnp.logical_not(is_mine(pairs_ref[0, pair]))
        task_ref[count] = pair
        return count + take.astype(jnp.int32)

    listed = lax.fori_loop(0, pair_count, list_pair, jnp.int32(per_block), unroll=8)

    def clear(slot, carry):
        task_ref[slot] = -1
        return carry

    lax.fori_loop(listed, slots + 1, clear, 0)

    for place in range(4):
        index = my_col + (place - 2)
        ok = (index >= 0) & (index < cols)
        block = gath_ref[jnp.clip(index, 0, cols - 1)]
        block = block.reshape(all_rows, columns).astype(jnp.float32)
        nat[:, place * columns : (place + 1) * columns] = jnp.where(ok, block, 0.0)

    row_of = lax.broadcasted_iota(jnp.int32, (LANES, LANES), 0)
    lane_of = lax.broadcasted_iota(jnp.int32, (LANES, LANES), 1)
    band = (
        ((row_of // rows) == (lane_of // rows)) & (jnp.abs(row_of - lane_of) <= RAD)
    ).astype(jnp.bfloat16)
    band_wide = jnp.concatenate([band, band], axis=1)
    band_tall = jnp.concatenate([band, band], axis=0)

    def across(sums):
        pair_sum = sums + pltpu.roll(sums, 1, 1)
        quad = pair_sum + pltpu.roll(pair_sum, 2, 1)
        octo = quad + pltpu.roll(quad, 4, 1)
        return pltpu.roll(octo + pltpu.roll(sums, 8, 1), wide - RAD, 1)

    for chunk in range(all_rows // LANES):
        span = slice(chunk * LANES, (chunk + 1) * LANES)
        tile = nat[span, :]
        nat_f[span, :] = pltpu.roll(tile, 2 * columns + RAD, 1)[:, : 2 * columns]
        mean = across(
            jnp.dot(band, tile.astype(jnp.bfloat16), preferred_element_type=jnp.float32)
        ) * scale
        high, low = split_exact(tile * tile)
        power = across(
            jnp.dot(
                band_wide, jnp.concatenate([high, low], axis=0), preferred_element_type=jnp.float32
            )
        ) * scale
        nat_m[span, :] = mean
        nat_r[span, :] = lax.rsqrt(power - mean * mean + SMOOTH)

    slot_lane = lax.broadcasted_iota(jnp.int32, (views * rows, LANES), 1)
    view_row = lax.broadcasted_iota(jnp.int32, (views * rows, LANES), 0)

    half = per_sub // 2
    three = 3 * columns
    target = view_row // rows
    same_row = lax.rem(slot_lane, rows) == lax.rem(view_row, rows)

    def prepare(batch, fold):
        first_of = jnp.full((views * rows, LANES), -1, jnp.int32)
        second_of = first_of
        for slot in range(per_batch):
            late = fold and 2 * slot >= per_batch
            pair = task_ref[batch * per_batch + (slot - per_batch // 2 if late else slot)]
            live = pair >= 0
            pair = jnp.maximum(pair, 0)
            first = pairs_ref[0, pair]
            second = pairs_ref[1, pair]
            first_at = pl.ds(pl.multiple_of(first * rows, rows), rows)
            second_at = pl.ds(pl.multiple_of(second * rows, rows), rows)
            here = slice(slot * rows, (slot + 1) * rows)
            start = 2 * columns - per_sub - RAD - offs_ref[pair] - sub_start
            if late:
                start = start - half
            turn = three - start
            st_g[here, :] = pltpu.roll(nat[second_at, :three], turn, 1)[:, : 2 * columns]
            st_m[here, :] = pltpu.roll(nat_m[second_at, :three], turn, 1)[:, : 2 * columns]
            st_r[here, :] = pltpu.roll(nat_r[second_at, :three], turn, 1)[:, : 2 * columns]
            st_f[here, :] = nat_f[first_at, :]
            st_a[here, :] = nat_m[first_at, 2 * columns : three]
            st_b[here, :] = nat_r[first_at, 2 * columns : three]
            mine = (slot_lane // rows) == slot
            first_of = jnp.where(mine, jnp.where(live, first - base, -1), first_of)
            second_of = jnp.where(mine, jnp.where(live, second - base, -1), second_of)
        hit = ((first_of == target) | (second_of == target)) & same_row
        early = slot_lane < LANES // 2
        for part in range(2):
            chosen = hit & (early if part == 0 else jnp.logical_not(early)) if fold else hit
            sel[part, batch] = chosen.astype(jnp.float32).astype(jnp.bfloat16)
        gt[batch] = st_g[...].T
        m2t[batch] = st_m[...].T
        r2t[batch] = st_r[...].T
        ft[batch] = st_f[...].T
        m1t[batch] = st_a[...].T * float(WIN * WIN)
        r1t[batch] = st_b[...].T * scale

    def prepare_full(batch, carry):
        prepare(batch, False)
        return carry

    lax.fori_loop(0, batches - int(folded), prepare_full, 0)
    if folded:
        prepare(batches - 1, True)

    span = columns + 2 * RAD
    work = [(batch, part) for part in range(2) for batch in range(batches)]
    if folded:
        work.remove((batches - 1, 1))

    def score(step, buffer):
        parts = []
        for batch, part in work:
            disp = step + part * half
            parts.append(
                split_exact(ft[batch, 0:span, :] * gt[batch, pl.ds(per_sub - disp, span), :])
            )
        stacked = jnp.concatenate([jnp.concatenate(pair, axis=1) for pair in parts], axis=0)
        sums = jnp.dot(stacked, band_tall, preferred_element_type=jnp.float32)
        costs = {}
        for unit, (batch, part) in enumerate(work):
            disp = step + part * half
            box_at, two_at, four_at = box.at[buffer, unit], two.at[buffer, unit], four.at[buffer, unit]
            one = sums[unit * span : (unit + 1) * span]
            box_at[0:span, :] = one
            pair_sum = one + box_at[1 : span + 1, :]
            two_at[0:span, :] = pair_sum
            quad = pair_sum + two_at[2 : span + 2, :]
            four_at[0:span, :] = quad
            cross = quad[0:columns] + four_at[4 : columns + 4, :] + one[2 * RAD :]
            at = pl.ds(per_sub + RAD - disp, columns)
            gain = r1t[batch] * r2t[batch, at, :]
            cost = 1.0 - (cross - m1t[batch] * m2t[batch, at, :]) * gain
            costs[batch, part] = cost.astype(jnp.bfloat16)
        for part in range(2):
            chosen = jnp.concatenate([sel[part, batch] for batch in range(batches)], axis=1)
            whole = jnp.concatenate(
                [costs.get((batch, part), costs[batch, 0]) for batch in range(batches)], axis=1
            )
            summed = lax.dot_general(
                chosen, whole, (((1,), (1,)), ((), ())), preferred_element_type=jnp.float32
            )
            out_ref[:, step + part * half] = summed.reshape(views, rows, columns)

    def score_steps(index, carry):
        for buffer in range(FOLD):
            score(index * FOLD + buffer, buffer)
        return carry

    lax.fori_loop(0, half // FOLD, score_steps, 0)


def per_device(images, pairs, offsets):
    views, rows, columns = images.shape
    blocks = lax.axis_size("views")
    cols = lax.axis_size("cols")
    per_sub = NDISP // lax.axis_size("sub")
    pair_count = pairs.shape[0]
    per_block = pair_count // blocks
    arriving = (2 * per_block // blocks) * (blocks - 1)
    per_batch = LANES // rows
    batches = -(-(per_block + arriving) // per_batch)
    folded = 2 * (batches * per_batch - per_block - arriving) >= per_batch
    units = 2 * batches - int(folded)
    gathered = gather_images(images.reshape(views * rows, columns), blocks, cols)
    dims = (blocks, cols, views, rows, columns, pair_count, per_sub, batches, folded)
    all_rows = blocks * views * rows
    span = columns + 2 * RAD
    f32 = jnp.float32
    stage = pltpu.VMEM((LANES, 2 * columns), f32)
    narrow = pltpu.VMEM((LANES, columns), f32)
    turned = pltpu.VMEM((batches, 2 * columns, LANES), f32)
    turned_narrow = pltpu.VMEM((batches, columns, LANES), f32)
    work = pltpu.VMEM((FOLD, units, span + 8, LANES), f32)
    whole = pltpu.VMEM((all_rows, 4 * columns), f32)
    smem = pl.BlockSpec(memory_space=pltpu.SMEM)
    vmem = pl.BlockSpec(memory_space=pltpu.VMEM)
    return pl.pallas_call(
        functools.partial(cost_kernel, dims),
        out_shape=jax.ShapeDtypeStruct((views, per_sub, rows, columns), f32),
        in_specs=[vmem, smem, smem],
        out_specs=vmem,
        scratch_shapes=[
            whole, pltpu.VMEM((all_rows, 2 * columns), f32), whole, whole,
            stage, stage, stage, stage, narrow, narrow,
            turned, turned, turned, turned, turned_narrow, turned_narrow,
            pltpu.VMEM((2, batches, views * rows, LANES), jnp.bfloat16),
            work, work, work,
            pltpu.SMEM((batches * per_batch + 1,), jnp.int32),
        ],
        compiler_params=pltpu.CompilerParams(vmem_limit_bytes=40 * 2**20),
    )(gathered, pairs.T, offsets)


def solution(mesh):
    return jax.shard_map(
        per_device,
        mesh=mesh,
        in_specs=(P(("groups", "views"), None, "cols"), P("groups", None), P("groups")),
        out_specs=P(("groups", "views"), "sub", None, "cols"),
        check_vma=False,
    )
```

```python
import functools

import jax
import jax.numpy as jnp
from jax import lax
from jax.experimental import pallas as pl
from jax.experimental.pallas import tpu as pltpu
from jax.sharding import PartitionSpec as P

NDISP = 64
RAD = 4
SMOOTH = 0.01
LANES = 128
FOLD = 2
WIN = 2 * RAD + 1
MESH = pl.DeviceIdType.MESH


def gather_kernel(blocks, cols, x_ref, out_ref, send_sem, recv_sem, own_sem):
    my_view = lax.axis_index("views")
    my_col = lax.axis_index("cols")
    me = my_view * cols + my_col
    total = blocks * cols

    def peer(step):
        other = lax.rem(me + step, total)
        return {"views": other // cols, "cols": lax.rem(other, cols)}

    own = pltpu.make_async_copy(x_ref, out_ref.at[my_col, my_view], own_sem)
    own.start()
    barrier = pltpu.get_barrier_semaphore()
    for step in range(1, total):
        pl.semaphore_signal(barrier, inc=1, device_id=peer(step), device_id_type=MESH)
    pl.semaphore_wait(barrier, total - 1)
    copies = []
    for step in range(1, total):
        copy = pltpu.make_async_remote_copy(
            src_ref=x_ref,
            dst_ref=out_ref.at[my_col, my_view],
            send_sem=send_sem.at[step],
            recv_sem=recv_sem.at[step],
            device_id=peer(step),
            device_id_type=MESH,
        )
        copy.start()
        copies.append(copy)
    own.wait()
    for copy in copies:
        copy.wait()


def gather_images(images, blocks, cols):
    rows, columns = images.shape
    total = blocks * cols
    return pl.pallas_call(
        functools.partial(gather_kernel, blocks, cols),
        out_shape=pltpu.VMEM((cols, blocks, rows, columns), images.dtype),
        in_specs=[pl.BlockSpec(memory_space=pltpu.VMEM)],
        out_specs=pl.BlockSpec(memory_space=pltpu.VMEM),
        scratch_shapes=[
            pltpu.SemaphoreType.DMA((total,)),
            pltpu.SemaphoreType.DMA((total,)),
            pltpu.SemaphoreType.DMA,
        ],
        compiler_params=pltpu.CompilerParams(collective_id=0, has_side_effects=True),
    )(images)


def split_exact(values):
    high = values.astype(jnp.bfloat16)
    low = (values - high.astype(jnp.float32)).astype(jnp.bfloat16)
    return high, low


def cost_kernel(
    dims, gath_ref, pairs_ref, offs_ref, out_ref,
    nat, nat_f, nat_m, nat_r, st_g, st_m, st_r, st_f, st_a, st_b,
    gt, m2t, r2t, ft, m1t, r1t, sel, box, two, task_ref,
):
    blocks, cols, views, rows, columns, pair_count, per_sub, batches, folded = dims
    per_batch = LANES // rows
    per_block = pair_count // blocks
    slots = batches * per_batch
    all_rows = blocks * views * rows
    wide = 4 * columns
    my_view = lax.axis_index("views")
    my_col = lax.axis_index("cols")
    sub_start = lax.axis_index("sub") * per_sub
    scale = 1.0 / float(WIN * WIN)

    base = my_view * views
    for slot in range(per_block):
        task_ref[slot] = my_view * per_block + slot

    def is_mine(view):
        return (view >= base) & (view < base + views)

    def list_pair(pair, count):
        take = is_mine(pairs_ref[1, pair]) & jnp.logical_not(is_mine(pairs_ref[0, pair]))
        task_ref[count] = pair
        return count + take.astype(jnp.int32)

    listed = lax.fori_loop(0, pair_count, list_pair, jnp.int32(per_block), unroll=8)

    def clear(slot, carry):
        task_ref[slot] = -1
        return carry

    lax.fori_loop(listed, slots + 1, clear, 0)

    for place in range(4):
        index = my_col + (place - 2)
        ok = (index >= 0) & (index < cols)
        block = gath_ref[jnp.clip(index, 0, cols - 1)]
        block = block.reshape(all_rows, columns).astype(jnp.float32)
        nat[:, place * columns : (place + 1) * columns] = jnp.where(ok, block, 0.0)

    row_of = lax.broadcasted_iota(jnp.int32, (LANES, LANES), 0)
    lane_of = lax.broadcasted_iota(jnp.int32, (LANES, LANES), 1)
    band = (
        ((row_of // rows) == (lane_of // rows)) & (jnp.abs(row_of - lane_of) <= RAD)
    ).astype(jnp.bfloat16)
    band_wide = jnp.concatenate([band, band], axis=1)
    band_tall = jnp.concatenate([band, band], axis=0)

    def across(sums):
        pair_sum = sums + pltpu.roll(sums, 1, 1)
        quad = pair_sum + pltpu.roll(pair_sum, 2, 1)
        octo = quad + pltpu.roll(quad, 4, 1)
        return pltpu.roll(octo + pltpu.roll(sums, 8, 1), wide - RAD, 1)

    for chunk in range(all_rows // LANES):
        span = slice(chunk * LANES, (chunk + 1) * LANES)
        tile = nat[span, :]
        nat_f[span, :] = pltpu.roll(tile, 2 * columns + RAD, 1)[:, : 2 * columns]
        mean = across(
            jnp.dot(band, tile.astype(jnp.bfloat16), preferred_element_type=jnp.float32)
        ) * scale
        high, low = split_exact(tile * tile)
        power = across(
            jnp.dot(
                band_wide, jnp.concatenate([high, low], axis=0), preferred_element_type=jnp.float32
            )
        ) * scale
        nat_m[span, :] = mean
        nat_r[span, :] = lax.rsqrt(power - mean * mean + SMOOTH)

    slot_lane = lax.broadcasted_iota(jnp.int32, (views * rows, LANES), 1)
    view_row = lax.broadcasted_iota(jnp.int32, (views * rows, LANES), 0)

    half = per_sub // 2
    three = 3 * columns
    target = view_row // rows
    same_row = lax.rem(slot_lane, rows) == lax.rem(view_row, rows)

    def prepare(batch, fold):
        first_of = jnp.full((views * rows, LANES), -1, jnp.int32)
        second_of = first_of
        for slot in range(per_batch):
            late = fold and 2 * slot >= per_batch
            pair = task_ref[batch * per_batch + (slot - per_batch // 2 if late else slot)]
            live = pair >= 0
            pair = jnp.maximum(pair, 0)
            first = pairs_ref[0, pair]
            second = pairs_ref[1, pair]
            first_at = pl.ds(pl.multiple_of(first * rows, rows), rows)
            second_at = pl.ds(pl.multiple_of(second * rows, rows), rows)
            here = slice(slot * rows, (slot + 1) * rows)
            start = 2 * columns - per_sub - RAD - offs_ref[pair] - sub_start
            if late:
                start = start - half
            turn = three - start
            st_g[here, :] = pltpu.roll(nat[second_at, :three], turn, 1)[:, : 2 * columns]
            st_m[here, :] = pltpu.roll(nat_m[second_at, :three], turn, 1)[:, : 2 * columns]
            st_r[here, :] = pltpu.roll(nat_r[second_at, :three], turn, 1)[:, : 2 * columns]
            st_f[here, :] = nat_f[first_at, :]
            st_a[here, :] = nat_m[first_at, 2 * columns : three]
            st_b[here, :] = nat_r[first_at, 2 * columns : three]
            mine = (slot_lane // rows) == slot
            first_of = jnp.where(mine, jnp.where(live, first - base, -1), first_of)
            second_of = jnp.where(mine, jnp.where(live, second - base, -1), second_of)
        hit = ((first_of == target) | (second_of == target)) & same_row
        early = slot_lane < LANES // 2
        for part in range(2):
            chosen = hit & (early if part == 0 else jnp.logical_not(early)) if fold else hit
            sel[part, batch] = chosen.astype(jnp.float32).astype(jnp.bfloat16)
        gt[batch] = st_g[...].T
        m2t[batch] = st_m[...].T
        r2t[batch] = st_r[...].T
        ft[batch] = st_f[...].T
        m1t[batch] = st_a[...].T * float(WIN * WIN)
        r1t[batch] = st_b[...].T * scale

    def prepare_full(batch, carry):
        prepare(batch, False)
        return carry

    lax.fori_loop(0, batches - int(folded), prepare_full, 0)
    if folded:
        prepare(batches - 1, True)

    span = columns + 2 * RAD
    work = [(batch, part) for part in range(2) for batch in range(batches)]
    if folded:
        work.remove((batches - 1, 1))

    def score(step, buffer):
        parts = []
        for batch, part in work:
            disp = step + part * half
            parts.append(
                split_exact(ft[batch, 0:span, :] * gt[batch, pl.ds(per_sub - disp, span), :])
            )
        stacked = jnp.concatenate([jnp.concatenate(pair, axis=1) for pair in parts], axis=0)
        sums = jnp.dot(stacked, band_tall, preferred_element_type=jnp.float32)
        costs = {}
        for unit, (batch, part) in enumerate(work):
            disp = step + part * half
            box_at, two_at = box.at[buffer, unit], two.at[buffer, unit]
            one = sums[unit * span : (unit + 1) * span]
            box_at[0:span, :] = one
            triple = one + box_at[1 : span + 1, :] + box_at[2 : span + 2, :]
            two_at[0:span, :] = triple
            cross = triple[0:columns] + two_at[3 : columns + 3, :] + two_at[6 : columns + 6, :]
            at = pl.ds(per_sub + RAD - disp, columns)
            gain = r1t[batch] * r2t[batch, at, :]
            cost = 1.0 - (cross - m1t[batch] * m2t[batch, at, :]) * gain
            costs[batch, part] = cost.astype(jnp.bfloat16)
        for part in range(2):
            chosen = jnp.concatenate([sel[part, batch] for batch in range(batches)], axis=1)
            whole = jnp.concatenate(
                [costs.get((batch, part), costs[batch, 0]) for batch in range(batches)], axis=1
            )
            summed = lax.dot_general(
                chosen, whole, (((1,), (1,)), ((), ())), preferred_element_type=jnp.float32
            )
            out_ref[:, step + part * half] = summed.reshape(views, rows, columns)

    def score_steps(index, carry):
        for buffer in range(FOLD):
            score(index * FOLD + buffer, buffer)
        return carry

    lax.fori_loop(0, half // FOLD, score_steps, 0)


def per_device(images, pairs, offsets):
    views, rows, columns = images.shape
    blocks = lax.axis_size("views")
    cols = lax.axis_size("cols")
    per_sub = NDISP // lax.axis_size("sub")
    pair_count = pairs.shape[0]
    per_block = pair_count // blocks
    arriving = (2 * per_block // blocks) * (blocks - 1)
    per_batch = LANES // rows
    batches = -(-(per_block + arriving) // per_batch)
    folded = 2 * (batches * per_batch - per_block - arriving) >= per_batch
    units = 2 * batches - int(folded)
    gathered = gather_images(images.reshape(views * rows, columns), blocks, cols)
    dims = (blocks, cols, views, rows, columns, pair_count, per_sub, batches, folded)
    all_rows = blocks * views * rows
    span = columns + 2 * RAD
    f32 = jnp.float32
    stage = pltpu.VMEM((LANES, 2 * columns), f32)
    narrow = pltpu.VMEM((LANES, columns), f32)
    turned = pltpu.VMEM((batches, 2 * columns, LANES), f32)
    turned_narrow = pltpu.VMEM((batches, columns, LANES), f32)
    work = pltpu.VMEM((FOLD, units, span + 8, LANES), f32)
    whole = pltpu.VMEM((all_rows, 4 * columns), f32)
    smem = pl.BlockSpec(memory_space=pltpu.SMEM)
    vmem = pl.BlockSpec(memory_space=pltpu.VMEM)
    return pl.pallas_call(
        functools.partial(cost_kernel, dims),
        out_shape=jax.ShapeDtypeStruct((views, per_sub, rows, columns), f32),
        in_specs=[vmem, smem, smem],
        out_specs=vmem,
        scratch_shapes=[
            whole, pltpu.VMEM((all_rows, 2 * columns), f32), whole, whole,
            stage, stage, stage, stage, narrow, narrow,
            turned, turned, turned, turned, turned_narrow, turned_narrow,
            pltpu.VMEM((2, batches, views * rows, LANES), jnp.bfloat16),
            work, work,
            pltpu.SMEM((batches * per_batch + 1,), jnp.int32),
        ],
        compiler_params=pltpu.CompilerParams(vmem_limit_bytes=40 * 2**20),
    )(gathered, pairs.T, offsets)


def solution(mesh):
    return jax.shard_map(
        per_device,
        mesh=mesh,
        in_specs=(P(("groups", "views"), None, "cols"), P("groups", None), P("groups")),
        out_specs=P(("groups", "views"), "sub", None, "cols"),
        check_vma=False,
    )
```

```python
import functools

import jax
import jax.numpy as jnp
from jax import lax
from jax.experimental import pallas as pl
from jax.experimental.pallas import tpu as pltpu
from jax.sharding import PartitionSpec as P

NDISP = 64
RAD = 4
SMOOTH = 0.01
LANES = 128
FOLD = 4
WIN = 2 * RAD + 1
MESH = pl.DeviceIdType.MESH


def gather_kernel(blocks, cols, x_ref, out_ref, send_sem, recv_sem, own_sem):
    my_view = lax.axis_index("views")
    my_col = lax.axis_index("cols")
    me = my_view * cols + my_col
    total = blocks * cols

    def peer(step):
        other = lax.rem(me + step, total)
        return {"views": other // cols, "cols": lax.rem(other, cols)}

    own = pltpu.make_async_copy(x_ref, out_ref.at[my_col, my_view], own_sem)
    own.start()
    barrier = pltpu.get_barrier_semaphore()
    for step in range(1, total):
        pl.semaphore_signal(barrier, inc=1, device_id=peer(step), device_id_type=MESH)
    pl.semaphore_wait(barrier, total - 1)
    copies = []
    for step in range(1, total):
        copy = pltpu.make_async_remote_copy(
            src_ref=x_ref,
            dst_ref=out_ref.at[my_col, my_view],
            send_sem=send_sem.at[step],
            recv_sem=recv_sem.at[step],
            device_id=peer(step),
            device_id_type=MESH,
        )
        copy.start()
        copies.append(copy)
    own.wait()
    for copy in copies:
        copy.wait()


def gather_images(images, blocks, cols):
    rows, columns = images.shape
    total = blocks * cols
    return pl.pallas_call(
        functools.partial(gather_kernel, blocks, cols),
        out_shape=pltpu.VMEM((cols, blocks, rows, columns), images.dtype),
        in_specs=[pl.BlockSpec(memory_space=pltpu.VMEM)],
        out_specs=pl.BlockSpec(memory_space=pltpu.VMEM),
        scratch_shapes=[
            pltpu.SemaphoreType.DMA((total,)),
            pltpu.SemaphoreType.DMA((total,)),
            pltpu.SemaphoreType.DMA,
        ],
        compiler_params=pltpu.CompilerParams(collective_id=0, has_side_effects=True),
    )(images)


def split_exact(values):
    high = values.astype(jnp.bfloat16)
    low = (values - high.astype(jnp.float32)).astype(jnp.bfloat16)
    return high, low


def cost_kernel(
    dims, gath_ref, pairs_ref, offs_ref, out_ref,
    nat, nat_f, nat_m, nat_r, st_g, st_m, st_r, st_f, st_a, st_b,
    gt, m2t, r2t, ft, m1t, r1t, sel, box, two, task_ref,
):
    blocks, cols, views, rows, columns, pair_count, per_sub, batches, folded = dims
    per_batch = LANES // rows
    per_block = pair_count // blocks
    slots = batches * per_batch
    all_rows = blocks * views * rows
    wide = 4 * columns
    three = 3 * columns
    my_view = lax.axis_index("views")
    my_col = lax.axis_index("cols")
    sub_start = lax.axis_index("sub") * per_sub
    scale = 1.0 / float(WIN * WIN)

    base = my_view * views
    for slot in range(per_block):
        task_ref[slot] = my_view * per_block + slot

    def is_mine(view):
        return (view >= base) & (view < base + views)

    def list_pair(pair, count):
        take = is_mine(pairs_ref[1, pair]) & jnp.logical_not(is_mine(pairs_ref[0, pair]))
        task_ref[count] = pair
        return count + take.astype(jnp.int32)

    listed = lax.fori_loop(0, pair_count, list_pair, jnp.int32(per_block), unroll=8)

    def clear(slot, carry):
        task_ref[slot] = -1
        return carry

    lax.fori_loop(listed, slots + 1, clear, 0)

    for place in range(4):
        index = my_col + (place - 2)
        ok = (index >= 0) & (index < cols)
        block = gath_ref[jnp.clip(index, 0, cols - 1)]
        block = block.reshape(all_rows, columns).astype(jnp.float32)
        nat[:, place * columns : (place + 1) * columns] = jnp.where(ok, block, 0.0)

    row_of = lax.broadcasted_iota(jnp.int32, (LANES, LANES), 0)
    lane_of = lax.broadcasted_iota(jnp.int32, (LANES, LANES), 1)
    band = (
        ((row_of // rows) == (lane_of // rows)) & (jnp.abs(row_of - lane_of) <= RAD)
    ).astype(jnp.bfloat16)
    band_wide = jnp.concatenate([band, band], axis=1)
    band_tall = jnp.concatenate([band, band], axis=0)

    def across(sums):
        pair_sum = sums + pltpu.roll(sums, 1, 1)
        quad = pair_sum + pltpu.roll(pair_sum, 2, 1)
        octo = quad + pltpu.roll(quad, 4, 1)
        return octo + pltpu.roll(sums, 8, 1)

    for chunk in range(all_rows // LANES):
        span = slice(chunk * LANES, (chunk + 1) * LANES)
        tile = pltpu.roll(nat[span, :], wide - RAD, 1)[:, :three]
        nat_f[span, :] = tile[:, columns:]
        mean = across(
            jnp.dot(band, tile.astype(jnp.bfloat16), preferred_element_type=jnp.float32)
        ) * scale
        high, low = split_exact(tile * tile)
        power = across(
            jnp.dot(
                band_wide, jnp.concatenate([high, low], axis=0), preferred_element_type=jnp.float32
            )
        ) * scale
        nat_m[span, :] = mean
        nat_r[span, :] = lax.rsqrt(power - mean * mean + SMOOTH)

    slot_lane = lax.broadcasted_iota(jnp.int32, (views * rows, LANES), 1)
    view_row = lax.broadcasted_iota(jnp.int32, (views * rows, LANES), 0)

    half = per_sub // 2
    target = view_row // rows
    same_row = lax.rem(slot_lane, rows) == lax.rem(view_row, rows)

    def prepare(batch, fold):
        first_of = jnp.full((views * rows, LANES), -1, jnp.int32)
        second_of = first_of
        for slot in range(per_batch):
            late = fold and 2 * slot >= per_batch
            pair = task_ref[batch * per_batch + (slot - per_batch // 2 if late else slot)]
            live = pair >= 0
            pair = jnp.maximum(pair, 0)
            first = pairs_ref[0, pair]
            second = pairs_ref[1, pair]
            first_at = pl.ds(pl.multiple_of(first * rows, rows), rows)
            second_at = pl.ds(pl.multiple_of(second * rows, rows), rows)
            here = slice(slot * rows, (slot + 1) * rows)
            start = 2 * columns - per_sub - RAD - offs_ref[pair] - sub_start
            if late:
                start = start - half
            turn = three - start
            st_g[here, :] = pltpu.roll(nat[second_at, :three], turn, 1)[:, : 2 * columns]
            st_m[here, :] = pltpu.roll(nat_m[second_at, :three], turn, 1)[:, : 2 * columns]
            st_r[here, :] = pltpu.roll(nat_r[second_at, :three], turn, 1)[:, : 2 * columns]
            st_f[here, :] = nat_f[first_at, :]
            st_a[here, :] = nat_m[first_at, 2 * columns : three]
            st_b[here, :] = nat_r[first_at, 2 * columns : three]
            mine = (slot_lane // rows) == slot
            first_of = jnp.where(mine, jnp.where(live, first - base, -1), first_of)
            second_of = jnp.where(mine, jnp.where(live, second - base, -1), second_of)
        hit = ((first_of == target) | (second_of == target)) & same_row
        early = slot_lane < LANES // 2
        for part in range(2):
            chosen = hit & (early if part == 0 else jnp.logical_not(early)) if fold else hit
            sel[part, batch] = chosen.astype(jnp.float32).astype(jnp.bfloat16)
        gt[batch] = st_g[...].T
        m2t[batch] = st_m[...].T
        r2t[batch] = st_r[...].T
        ft[batch] = st_f[...].T
        m1t[batch] = st_a[...].T * float(WIN * WIN)
        r1t[batch] = st_b[...].T * scale

    def prepare_full(batch, carry):
        prepare(batch, False)
        return carry

    lax.fori_loop(0, batches - int(folded), prepare_full, 0)
    if folded:
        prepare(batches - 1, True)

    span = columns + 2 * RAD
    work = [(batch, part) for part in range(2) for batch in range(batches)]
    if folded:
        work.remove((batches - 1, 1))

    def score(step, buffer):
        parts = []
        for batch, part in work:
            disp = step + part * half
            parts.append(
                split_exact(ft[batch, 2 * columns - span :, :] * gt[batch, pl.ds(per_sub - disp, span), :])
            )
        stacked = jnp.concatenate([jnp.concatenate(pair, axis=1) for pair in parts], axis=0)
        sums = jnp.dot(stacked, band_tall, preferred_element_type=jnp.float32)
        costs = {}
        for unit, (batch, part) in enumerate(work):
            disp = step + part * half
            box_at, two_at = box.at[buffer, unit], two.at[buffer, unit]
            one = sums[unit * span : (unit + 1) * span]
            box_at[0:span, :] = one
            triple = one + box_at[1 : span + 1, :] + box_at[2 : span + 2, :]
            two_at[0:span, :] = triple
            cross = triple[0:columns] + two_at[3 : columns + 3, :] + two_at[6 : columns + 6, :]
            at = pl.ds(per_sub + RAD - disp, columns)
            gain = r1t[batch] * r2t[batch, at, :]
            cost = 1.0 - (cross - m1t[batch] * m2t[batch, at, :]) * gain
            costs[batch, part] = cost.astype(jnp.bfloat16)
        for part in range(2):
            chosen = jnp.concatenate([sel[part, batch] for batch in range(batches)], axis=1)
            whole = jnp.concatenate(
                [costs.get((batch, part), costs[batch, 0]) for batch in range(batches)], axis=1
            )
            summed = lax.dot_general(
                chosen, whole, (((1,), (1,)), ((), ())), preferred_element_type=jnp.float32
            )
            out_ref[:, step + part * half] = summed.reshape(views, rows, columns)

    def score_steps(index, carry):
        for buffer in range(FOLD):
            score(index * FOLD + buffer, buffer)
        return carry

    lax.fori_loop(0, half // FOLD, score_steps, 0)


def per_device(images, pairs, offsets):
    views, rows, columns = images.shape
    blocks = lax.axis_size("views")
    cols = lax.axis_size("cols")
    per_sub = NDISP // lax.axis_size("sub")
    pair_count = pairs.shape[0]
    per_block = pair_count // blocks
    arriving = (2 * per_block // blocks) * (blocks - 1)
    per_batch = LANES // rows
    batches = -(-(per_block + arriving) // per_batch)
    folded = 2 * (batches * per_batch - per_block - arriving) >= per_batch
    units = 2 * batches - int(folded)
    gathered = gather_images(images.reshape(views * rows, columns), blocks, cols)
    dims = (blocks, cols, views, rows, columns, pair_count, per_sub, batches, folded)
    all_rows = blocks * views * rows
    span = columns + 2 * RAD
    f32 = jnp.float32
    stage = pltpu.VMEM((LANES, 2 * columns), f32)
    narrow = pltpu.VMEM((LANES, columns), f32)
    turned = pltpu.VMEM((batches, 2 * columns, LANES), f32)
    turned_narrow = pltpu.VMEM((batches, columns, LANES), f32)
    work = pltpu.VMEM((FOLD, units, span + 8, LANES), f32)
    whole = pltpu.VMEM((all_rows, 4 * columns), f32)
    trio = pltpu.VMEM((all_rows, 3 * columns), f32)
    smem = pl.BlockSpec(memory_space=pltpu.SMEM)
    vmem = pl.BlockSpec(memory_space=pltpu.VMEM)
    return pl.pallas_call(
        functools.partial(cost_kernel, dims),
        out_shape=jax.ShapeDtypeStruct((views, per_sub, rows, columns), f32),
        in_specs=[vmem, smem, smem],
        out_specs=vmem,
        scratch_shapes=[
            whole, pltpu.VMEM((all_rows, 2 * columns), f32), trio, trio,
            stage, stage, stage, stage, narrow, narrow,
            turned, turned, turned, turned, turned_narrow, turned_narrow,
            pltpu.VMEM((2, batches, views * rows, LANES), jnp.bfloat16),
            work, work,
            pltpu.SMEM((batches * per_batch + 1,), jnp.int32),
        ],
        compiler_params=pltpu.CompilerParams(vmem_limit_bytes=40 * 2**20),
    )(gathered, pairs.T, offsets)


def solution(mesh):
    return jax.shard_map(
        per_device,
        mesh=mesh,
        in_specs=(P(("groups", "views"), None, "cols"), P("groups", None), P("groups")),
        out_specs=P(("groups", "views"), "sub", None, "cols"),
        check_vma=False,
    )
```

```python
import functools

import jax
import jax.numpy as jnp
from jax import lax
from jax.experimental import pallas as pl
from jax.experimental.pallas import tpu as pltpu
from jax.sharding import PartitionSpec as P

NDISP = 64
RAD = 4
SMOOTH = 0.01
LANES = 128
FOLD = 4
WIN = 2 * RAD + 1
MESH = pl.DeviceIdType.MESH


def gather_kernel(blocks, cols, x_ref, out_ref, send_sem, recv_sem, own_sem):
    my_view = lax.axis_index("views")
    my_col = lax.axis_index("cols")
    me = my_view * cols + my_col
    total = blocks * cols

    def peer(step):
        other = lax.rem(me + step, total)
        return {"views": other // cols, "cols": lax.rem(other, cols)}

    own = pltpu.make_async_copy(x_ref, out_ref.at[my_col, my_view], own_sem)
    own.start()
    barrier = pltpu.get_barrier_semaphore()
    for step in range(1, total):
        pl.semaphore_signal(barrier, inc=1, device_id=peer(step), device_id_type=MESH)
    pl.semaphore_wait(barrier, total - 1)
    copies = []
    for step in range(1, total):
        copy = pltpu.make_async_remote_copy(
            src_ref=x_ref,
            dst_ref=out_ref.at[my_col, my_view],
            send_sem=send_sem.at[step],
            recv_sem=recv_sem.at[step],
            device_id=peer(step),
            device_id_type=MESH,
        )
        copy.start()
        copies.append(copy)
    own.wait()
    for copy in copies:
        copy.wait()


def gather_images(images, blocks, cols):
    rows, columns = images.shape
    total = blocks * cols
    return pl.pallas_call(
        functools.partial(gather_kernel, blocks, cols),
        out_shape=pltpu.VMEM((cols, blocks, rows, columns), images.dtype),
        in_specs=[pl.BlockSpec(memory_space=pltpu.VMEM)],
        out_specs=pl.BlockSpec(memory_space=pltpu.VMEM),
        scratch_shapes=[
            pltpu.SemaphoreType.DMA((total,)),
            pltpu.SemaphoreType.DMA((total,)),
            pltpu.SemaphoreType.DMA,
        ],
        compiler_params=pltpu.CompilerParams(collective_id=0, has_side_effects=True),
    )(images)


def split_exact(values):
    high = values.astype(jnp.bfloat16)
    low = (values - high.astype(jnp.float32)).astype(jnp.bfloat16)
    return high, low


def cost_kernel(
    dims, gath_ref, pairs_ref, offs_ref, out_ref,
    nat, nat_f, nat_m, nat_r, st_g, st_m, st_r, st_f, st_a, st_b,
    gt, m2t, r2t, ft, m1t, r1t, sel, box, two, task_ref,
):
    blocks, cols, views, rows, columns, pair_count, per_sub, batches, folded = dims
    per_batch = LANES // rows
    per_block = pair_count // blocks
    slots = batches * per_batch
    all_rows = blocks * views * rows
    wide = 4 * columns
    three = 3 * columns
    my_view = lax.axis_index("views")
    my_col = lax.axis_index("cols")
    sub_start = lax.axis_index("sub") * per_sub
    scale = 1.0 / float(WIN * WIN)

    base = my_view * views
    for slot in range(per_block):
        task_ref[slot] = my_view * per_block + slot

    def is_mine(view):
        return (view >= base) & (view < base + views)

    def list_pair(pair, count):
        take = is_mine(pairs_ref[1, pair]) & jnp.logical_not(is_mine(pairs_ref[0, pair]))
        task_ref[count] = pair
        return count + take.astype(jnp.int32)

    listed = lax.fori_loop(0, pair_count, list_pair, jnp.int32(per_block), unroll=8)

    def clear(slot, carry):
        task_ref[slot] = -1
        return carry

    lax.fori_loop(listed, slots + 1, clear, 0)

    for place in range(4):
        index = my_col + (place - 2)
        ok = (index >= 0) & (index < cols)
        block = gath_ref[jnp.clip(index, 0, cols - 1)]
        block = block.reshape(all_rows, columns).astype(jnp.float32)
        nat[:, place * columns : (place + 1) * columns] = jnp.where(ok, block, 0.0)

    row_of = lax.broadcasted_iota(jnp.int32, (LANES, LANES), 0)
    lane_of = lax.broadcasted_iota(jnp.int32, (LANES, LANES), 1)
    band = (
        ((row_of // rows) == (lane_of // rows)) & (jnp.abs(row_of - lane_of) <= RAD)
    ).astype(jnp.bfloat16)
    band_wide = jnp.concatenate([band, band], axis=1)
    band_tall = jnp.concatenate([band, band], axis=0)

    def across(sums):
        pair_sum = sums + pltpu.roll(sums, 1, 1)
        quad = pair_sum + pltpu.roll(pair_sum, 2, 1)
        octo = quad + pltpu.roll(quad, 4, 1)
        return octo + pltpu.roll(sums, 8, 1)

    for chunk in range(all_rows // LANES):
        span = slice(chunk * LANES, (chunk + 1) * LANES)
        tile = pltpu.roll(nat[span, :], wide - RAD, 1)[:, :three]
        nat_f[span, :] = tile[:, columns:]
        mean = across(
            jnp.dot(band, tile.astype(jnp.bfloat16), preferred_element_type=jnp.float32)
        ) * scale
        high, low = split_exact(tile * tile)
        power = across(
            jnp.dot(
                band_wide, jnp.concatenate([high, low], axis=0), preferred_element_type=jnp.float32
            )
        ) * scale
        nat_m[span, :] = mean
        nat_r[span, :] = lax.rsqrt(power - mean * mean + SMOOTH)

    slot_lane = lax.broadcasted_iota(jnp.int32, (views * rows, LANES), 1)
    view_row = lax.broadcasted_iota(jnp.int32, (views * rows, LANES), 0)

    half = per_sub // 2
    target = view_row // rows
    same_row = lax.rem(slot_lane, rows) == lax.rem(view_row, rows)

    def prepare(batch, fold):
        first_of = jnp.full((views * rows, LANES), -1, jnp.int32)
        second_of = first_of
        for slot in range(per_batch):
            late = fold and 2 * slot >= per_batch
            pair = task_ref[batch * per_batch + (slot - per_batch // 2 if late else slot)]
            live = pair >= 0
            pair = jnp.maximum(pair, 0)
            first = pairs_ref[0, pair]
            second = pairs_ref[1, pair]
            first_at = pl.ds(pl.multiple_of(first * rows, rows), rows)
            second_at = pl.ds(pl.multiple_of(second * rows, rows), rows)
            here = slice(slot * rows, (slot + 1) * rows)
            start = 2 * columns - per_sub - RAD - offs_ref[pair] - sub_start
            if late:
                start = start - half
            turn = three - start
            st_g[batch, here, :] = pltpu.roll(nat[second_at, :three], turn, 1)[:, : 2 * columns]
            st_m[batch, here, :] = pltpu.roll(nat_m[second_at, :three], turn, 1)[:, : 2 * columns]
            st_r[batch, here, :] = pltpu.roll(nat_r[second_at, :three], turn, 1)[:, : 2 * columns]
            st_f[batch, here, :] = nat_f[first_at, :]
            st_a[batch, here, :] = nat_m[first_at, 2 * columns : three]
            st_b[batch, here, :] = nat_r[first_at, 2 * columns : three]
            mine = (slot_lane // rows) == slot
            first_of = jnp.where(mine, jnp.where(live, first - base, -1), first_of)
            second_of = jnp.where(mine, jnp.where(live, second - base, -1), second_of)
        hit = ((first_of == target) | (second_of == target)) & same_row
        early = slot_lane < LANES // 2
        for part in range(2):
            chosen = hit & (early if part == 0 else jnp.logical_not(early)) if fold else hit
            sel[part, batch] = chosen.astype(jnp.float32).astype(jnp.bfloat16)
        gt[batch] = st_g[batch].T
        m2t[batch] = st_m[batch].T
        r2t[batch] = st_r[batch].T
        ft[batch] = st_f[batch].T
        m1t[batch] = st_a[batch].T * float(WIN * WIN)
        r1t[batch] = st_b[batch].T * scale

    for batch in range(batches):
        prepare(batch, folded and batch == batches - 1)

    span = columns + 2 * RAD
    work = [(batch, part) for part in range(2) for batch in range(batches)]
    if folded:
        work.remove((batches - 1, 1))

    def score(step, buffer):
        parts = []
        for batch, part in work:
            disp = step + part * half
            parts.append(
                split_exact(ft[batch, 2 * columns - span :, :] * gt[batch, pl.ds(per_sub - disp, span), :])
            )
        costs = {}
        for unit, (batch, part) in enumerate(work):
            disp = step + part * half
            box_at, two_at = box.at[buffer, unit], two.at[buffer, unit]
            one = jnp.dot(
                jnp.concatenate(parts[unit], axis=1), band_tall, preferred_element_type=jnp.float32
            )
            box_at[0:span, :] = one
            triple = one + box_at[1 : span + 1, :] + box_at[2 : span + 2, :]
            two_at[0:span, :] = triple
            cross = triple[0:columns] + two_at[3 : columns + 3, :] + two_at[6 : columns + 6, :]
            at = pl.ds(per_sub + RAD - disp, columns)
            gain = r1t[batch] * r2t[batch, at, :]
            cost = 1.0 - (cross - m1t[batch] * m2t[batch, at, :]) * gain
            costs[batch, part] = cost.astype(jnp.bfloat16)
        for part in range(2):
            chosen = jnp.concatenate([sel[part, batch] for batch in range(batches)], axis=1)
            whole = jnp.concatenate(
                [costs.get((batch, part), costs[batch, 0]) for batch in range(batches)], axis=1
            )
            summed = lax.dot_general(
                chosen, whole, (((1,), (1,)), ((), ())), preferred_element_type=jnp.float32
            )
            out_ref[:, step + part * half] = summed.reshape(views, rows, columns)

    def score_steps(index, carry):
        for buffer in range(FOLD):
            score(index * FOLD + buffer, buffer)
        return carry

    lax.fori_loop(0, half // FOLD, score_steps, 0)


def per_device(images, pairs, offsets):
    views, rows, columns = images.shape
    blocks = lax.axis_size("views")
    cols = lax.axis_size("cols")
    per_sub = NDISP // lax.axis_size("sub")
    pair_count = pairs.shape[0]
    per_block = pair_count // blocks
    arriving = (2 * per_block // blocks) * (blocks - 1)
    per_batch = LANES // rows
    batches = -(-(per_block + arriving) // per_batch)
    folded = 2 * (batches * per_batch - per_block - arriving) >= per_batch
    units = 2 * batches - int(folded)
    gathered = gather_images(images.reshape(views * rows, columns), blocks, cols)
    dims = (blocks, cols, views, rows, columns, pair_count, per_sub, batches, folded)
    all_rows = blocks * views * rows
    span = columns + 2 * RAD
    f32 = jnp.float32
    stage = pltpu.VMEM((batches, LANES, 2 * columns), f32)
    narrow = pltpu.VMEM((batches, LANES, columns), f32)
    turned = pltpu.VMEM((batches, 2 * columns, LANES), f32)
    turned_narrow = pltpu.VMEM((batches, columns, LANES), f32)
    work = pltpu.VMEM((FOLD, units, span + 8, LANES), f32)
    whole = pltpu.VMEM((all_rows, 4 * columns), f32)
    trio = pltpu.VMEM((all_rows, 3 * columns), f32)
    smem = pl.BlockSpec(memory_space=pltpu.SMEM)
    vmem = pl.BlockSpec(memory_space=pltpu.VMEM)
    return pl.pallas_call(
        functools.partial(cost_kernel, dims),
        out_shape=jax.ShapeDtypeStruct((views, per_sub, rows, columns), f32),
        in_specs=[vmem, smem, smem],
        out_specs=vmem,
        scratch_shapes=[
            whole, pltpu.VMEM((all_rows, 2 * columns), f32), trio, trio,
            stage, stage, stage, stage, narrow, narrow,
            turned, turned, turned, turned, turned_narrow, turned_narrow,
            pltpu.VMEM((2, batches, views * rows, LANES), jnp.bfloat16),
            work, work,
            pltpu.SMEM((batches * per_batch + 1,), jnp.int32),
        ],
        compiler_params=pltpu.CompilerParams(vmem_limit_bytes=40 * 2**20),
    )(gathered, pairs.T, offsets)


def solution(mesh):
    return jax.shard_map(
        per_device,
        mesh=mesh,
        in_specs=(P(("groups", "views"), None, "cols"), P("groups", None), P("groups")),
        out_specs=P(("groups", "views"), "sub", None, "cols"),
        check_vma=False,
    )
```

```python
import functools

import jax
import jax.numpy as jnp
from jax import lax
from jax.experimental import pallas as pl
from jax.experimental.pallas import tpu as pltpu
from jax.sharding import PartitionSpec as P

NDISP = 64
RAD = 4
SMOOTH = 0.01
LANES = 128
FOLD = 8
WIN = 2 * RAD + 1
MESH = pl.DeviceIdType.MESH


def gather_kernel(blocks, cols, x_ref, out_ref, send_sem, recv_sem, own_sem):
    my_view = lax.axis_index("views")
    my_col = lax.axis_index("cols")
    me = my_view * cols + my_col
    total = blocks * cols

    def peer(step):
        other = lax.rem(me + step, total)
        return {"views": other // cols, "cols": lax.rem(other, cols)}

    own = pltpu.make_async_copy(x_ref, out_ref.at[my_col, my_view], own_sem)
    own.start()
    barrier = pltpu.get_barrier_semaphore()
    for step in range(1, total):
        pl.semaphore_signal(barrier, inc=1, device_id=peer(step), device_id_type=MESH)
    pl.semaphore_wait(barrier, total - 1)
    copies = []
    for step in range(1, total):
        copy = pltpu.make_async_remote_copy(
            src_ref=x_ref,
            dst_ref=out_ref.at[my_col, my_view],
            send_sem=send_sem.at[step],
            recv_sem=recv_sem.at[step],
            device_id=peer(step),
            device_id_type=MESH,
        )
        copy.start()
        copies.append(copy)
    own.wait()
    for copy in copies:
        copy.wait()


def gather_images(images, blocks, cols):
    rows, columns = images.shape
    total = blocks * cols
    return pl.pallas_call(
        functools.partial(gather_kernel, blocks, cols),
        out_shape=pltpu.VMEM((cols, blocks, rows, columns), images.dtype),
        in_specs=[pl.BlockSpec(memory_space=pltpu.VMEM)],
        out_specs=pl.BlockSpec(memory_space=pltpu.VMEM),
        scratch_shapes=[
            pltpu.SemaphoreType.DMA((total,)),
            pltpu.SemaphoreType.DMA((total,)),
            pltpu.SemaphoreType.DMA,
        ],
        compiler_params=pltpu.CompilerParams(collective_id=0, has_side_effects=True),
    )(images)


def split_exact(values):
    high = values.astype(jnp.bfloat16)
    low = (values - high.astype(jnp.float32)).astype(jnp.bfloat16)
    return high, low


def cost_kernel(
    dims, gath_ref, pairs_ref, offs_ref, out_ref,
    nat, nat_f, nat_m, nat_r, st_g, st_m, st_r, st_f, st_a, st_b,
    gt, m2t, r2t, ft, m1t, r1t, sel, box, two, task_ref,
):
    blocks, cols, views, rows, columns, pair_count, per_sub, batches, folded = dims
    per_batch = LANES // rows
    per_block = pair_count // blocks
    slots = batches * per_batch
    all_rows = blocks * views * rows
    wide = 4 * columns
    three = 3 * columns
    my_view = lax.axis_index("views")
    my_col = lax.axis_index("cols")
    sub_start = lax.axis_index("sub") * per_sub
    scale = 1.0 / float(WIN * WIN)

    base = my_view * views
    for slot in range(per_block):
        task_ref[slot] = my_view * per_block + slot

    def is_mine(view):
        return (view >= base) & (view < base + views)

    def list_pair(pair, count):
        take = is_mine(pairs_ref[1, pair]) & jnp.logical_not(is_mine(pairs_ref[0, pair]))
        task_ref[count] = pair
        return count + take.astype(jnp.int32)

    listed = lax.fori_loop(0, pair_count, list_pair, jnp.int32(per_block), unroll=8)

    def clear(slot, carry):
        task_ref[slot] = -1
        return carry

    lax.fori_loop(listed, slots + 1, clear, 0)

    for place in range(4):
        index = my_col + (place - 2)
        ok = (index >= 0) & (index < cols)
        block = gath_ref[jnp.clip(index, 0, cols - 1)]
        block = block.reshape(all_rows, columns).astype(jnp.float32)
        nat[:, place * columns : (place + 1) * columns] = jnp.where(ok, block, 0.0)

    row_of = lax.broadcasted_iota(jnp.int32, (LANES, LANES), 0)
    lane_of = lax.broadcasted_iota(jnp.int32, (LANES, LANES), 1)
    band = (
        ((row_of // rows) == (lane_of // rows)) & (jnp.abs(row_of - lane_of) <= RAD)
    ).astype(jnp.bfloat16)
    band_wide = jnp.concatenate([band, band], axis=1)
    band_tall = jnp.concatenate([band, band], axis=0)

    def across(sums):
        pair_sum = sums + pltpu.roll(sums, 1, 1)
        quad = pair_sum + pltpu.roll(pair_sum, 2, 1)
        octo = quad + pltpu.roll(quad, 4, 1)
        return octo + pltpu.roll(sums, 8, 1)

    for chunk in range(all_rows // LANES):
        span = slice(chunk * LANES, (chunk + 1) * LANES)
        tile = pltpu.roll(nat[span, :], wide - RAD, 1)[:, :three]
        nat_f[span, :] = tile[:, columns:]
        mean = across(
            jnp.dot(band, tile.astype(jnp.bfloat16), preferred_element_type=jnp.float32)
        ) * scale
        high, low = split_exact(tile * tile)
        power = across(
            jnp.dot(
                band_wide, jnp.concatenate([high, low], axis=0), preferred_element_type=jnp.float32
            )
        ) * scale
        nat_m[span, :] = mean
        nat_r[span, :] = lax.rsqrt(power - mean * mean + SMOOTH)

    slot_lane = lax.broadcasted_iota(jnp.int32, (views * rows, LANES), 1)
    view_row = lax.broadcasted_iota(jnp.int32, (views * rows, LANES), 0)

    half = per_sub // 2
    target = view_row // rows
    same_row = lax.rem(slot_lane, rows) == lax.rem(view_row, rows)

    def prepare(batch, fold):
        first_of = jnp.full((views * rows, LANES), -1, jnp.int32)
        second_of = first_of
        for slot in range(per_batch):
            late = fold and 2 * slot >= per_batch
            pair = task_ref[batch * per_batch + (slot - per_batch // 2 if late else slot)]
            live = pair >= 0
            pair = jnp.maximum(pair, 0)
            first = pairs_ref[0, pair]
            second = pairs_ref[1, pair]
            first_at = pl.ds(pl.multiple_of(first * rows, rows), rows)
            second_at = pl.ds(pl.multiple_of(second * rows, rows), rows)
            here = slice(slot * rows, (slot + 1) * rows)
            start = 2 * columns - per_sub - RAD - offs_ref[pair] - sub_start
            if late:
                start = start - half
            turn = three - start
            st_g[batch, here, :] = pltpu.roll(nat[second_at, :three], turn, 1)[:, : 2 * columns]
            st_m[batch, here, :] = pltpu.roll(nat_m[second_at, :three], turn, 1)[:, : 2 * columns]
            st_r[batch, here, :] = pltpu.roll(nat_r[second_at, :three], turn, 1)[:, : 2 * columns]
            st_f[batch, here, :] = nat_f[first_at, :]
            st_a[batch, here, :] = nat_m[first_at, 2 * columns : three]
            st_b[batch, here, :] = nat_r[first_at, 2 * columns : three]
            mine = (slot_lane // rows) == slot
            first_of = jnp.where(mine, jnp.where(live, first - base, -1), first_of)
            second_of = jnp.where(mine, jnp.where(live, second - base, -1), second_of)
        hit = ((first_of == target) | (second_of == target)) & same_row
        early = slot_lane < LANES // 2
        for part in range(2):
            chosen = hit & (early if part == 0 else jnp.logical_not(early)) if fold else hit
            sel[part, batch] = chosen.astype(jnp.float32).astype(jnp.bfloat16)
        gt[batch] = st_g[batch].T
        m2t[batch] = st_m[batch].T
        r2t[batch] = st_r[batch].T
        ft[batch] = st_f[batch].T
        m1t[batch] = st_a[batch].T * float(WIN * WIN)
        r1t[batch] = st_b[batch].T * scale

    for batch in range(batches):
        prepare(batch, folded and batch == batches - 1)

    span = columns + 2 * RAD
    work = [(batch, part) for part in range(2) for batch in range(batches)]
    if folded:
        work.remove((batches - 1, 1))

    def score(step, buffer):
        costs = {}
        for unit, (batch, part) in enumerate(work):
            disp = step + part * half
            box_at, two_at = box.at[buffer, unit], two.at[buffer, unit]
            product = ft[batch, 2 * columns - span :, :] * gt[batch, pl.ds(per_sub - disp, span), :]
            one = jnp.dot(
                jnp.concatenate(split_exact(product), axis=1), band_tall, preferred_element_type=jnp.float32
            )
            box_at[0:span, :] = one
            triple = one + box_at[1 : span + 1, :] + box_at[2 : span + 2, :]
            two_at[0:span, :] = triple
            cross = triple[0:columns] + two_at[3 : columns + 3, :] + two_at[6 : columns + 6, :]
            at = pl.ds(per_sub + RAD - disp, columns)
            gain = r1t[batch] * r2t[batch, at, :]
            cost = 1.0 - (cross - m1t[batch] * m2t[batch, at, :]) * gain
            costs[batch, part] = cost.astype(jnp.bfloat16)
        for part in range(2):
            chosen = jnp.concatenate([sel[part, batch] for batch in range(batches)], axis=1)
            whole = jnp.concatenate(
                [costs.get((batch, part), costs[batch, 0]) for batch in range(batches)], axis=1
            )
            summed = lax.dot_general(
                chosen, whole, (((1,), (1,)), ((), ())), preferred_element_type=jnp.float32
            )
            out_ref[:, step + part * half] = summed.reshape(views, rows, columns)

    def score_steps(index, carry):
        for buffer in range(FOLD):
            score(index * FOLD + buffer, buffer)
        return carry

    lax.fori_loop(0, half // FOLD, score_steps, 0)


def per_device(images, pairs, offsets):
    views, rows, columns = images.shape
    blocks = lax.axis_size("views")
    cols = lax.axis_size("cols")
    per_sub = NDISP // lax.axis_size("sub")
    pair_count = pairs.shape[0]
    per_block = pair_count // blocks
    arriving = (2 * per_block // blocks) * (blocks - 1)
    per_batch = LANES // rows
    batches = -(-(per_block + arriving) // per_batch)
    folded = 2 * (batches * per_batch - per_block - arriving) >= per_batch
    units = 2 * batches - int(folded)
    gathered = gather_images(images.reshape(views * rows, columns), blocks, cols)
    dims = (blocks, cols, views, rows, columns, pair_count, per_sub, batches, folded)
    all_rows = blocks * views * rows
    span = columns + 2 * RAD
    f32 = jnp.float32
    stage = pltpu.VMEM((batches, LANES, 2 * columns), f32)
    narrow = pltpu.VMEM((batches, LANES, columns), f32)
    turned = pltpu.VMEM((batches, 2 * columns, LANES), f32)
    turned_narrow = pltpu.VMEM((batches, columns, LANES), f32)
    work = pltpu.VMEM((FOLD, units, span + 8, LANES), f32)
    whole = pltpu.VMEM((all_rows, 4 * columns), f32)
    trio = pltpu.VMEM((all_rows, 3 * columns), f32)
    smem = pl.BlockSpec(memory_space=pltpu.SMEM)
    vmem = pl.BlockSpec(memory_space=pltpu.VMEM)
    return pl.pallas_call(
        functools.partial(cost_kernel, dims),
        out_shape=jax.ShapeDtypeStruct((views, per_sub, rows, columns), f32),
        in_specs=[vmem, smem, smem],
        out_specs=vmem,
        scratch_shapes=[
            whole, pltpu.VMEM((all_rows, 2 * columns), f32), trio, trio,
            stage, stage, stage, stage, narrow, narrow,
            turned, turned, turned, turned, turned_narrow, turned_narrow,
            pltpu.VMEM((2, batches, views * rows, LANES), jnp.bfloat16),
            work, work,
            pltpu.SMEM((batches * per_batch + 1,), jnp.int32),
        ],
        compiler_params=pltpu.CompilerParams(vmem_limit_bytes=40 * 2**20),
    )(gathered, pairs.T, offsets)


def solution(mesh):
    return jax.shard_map(
        per_device,
        mesh=mesh,
        in_specs=(P(("groups", "views"), None, "cols"), P("groups", None), P("groups")),
        out_specs=P(("groups", "views"), "sub", None, "cols"),
        check_vma=False,
    )
```
